512 devices in a mesh: gx: 8 (over y), gy: 8 (over z), gz: 8 (over x, core).
Axes of the slice: x: 4, y: 8, z: 8, core: 2. Of those that a mesh axis runs over, the one named last changes fastest.
Arguments:
- point_offset: float32 [3, 8, 8, 8, 128, 128], P(None, 'gx', 'gy', 'gz'), may hold values from 0 to 1
- point_mass: float32 [8, 8, 8, 128, 128], P('gx', 'gy', 'gz'), may hold values from 0.3 to 3
- point_velocity: float32 [3, 8, 8, 8, 128, 128], P(None, 'gx', 'gy', 'gz'), may hold values from -6 to 6
- point_stiffness: float32 [8, 8, 8, 128, 128], P('gx', 'gy', 'gz'), may hold values from 0.1 to 2
- cell_index: int32 [8, 8, 8, 128], P('gx', 'gy', 'gz'), may hold values from 0 to 8191, as said below
- live_count: int32 [8, 8, 8, 128], P('gx', 'gy', 'gz'), may hold values from 1 to 128
Outputs:
- grid_velocity: float32 [3, 64, 64, 1024], P(None, 'gx', 'gy', 'gz')
- point_update: float32 [3, 8, 8, 8, 128, 128], P(None, 'gx', 'gy', 'gz')
The draws below stay inside these ranges and needn't reach their ends.
Inputs may be any that keep to these rules, and one draw needn't show every extreme that they name: `cell_index`: every value from 0 to 8191 may occur, several blocks may share a cell.
All inputs are finite; a program needn't handle non-finite values.
Results may differ from the reference program's by a relative error of at most 0.0003.
Values sent between devices are 32-bit elements; how exact they have to be, the bound alone decides.
A program may use at most 64 MiB of HBM per device.

```python
import math
import jax
import jax.numpy as jnp
from jax import lax

CX = 8
CY = 8
CZ = 128
NB = 128
PTS = 128
NEWTON = 2
CG = 4
NX = 64
NY = 64
NZ = 1024
N_GX = 8
N_GY = 8
N_GZ = 8


def draw_cell_index(key, part):
    key = jax.random.fold_in(key, 11)
    cells = jax.random.randint(key, (N_GX, N_GY, N_GZ, NB), 0, CX * CY * CZ, dtype=jnp.int32)
    cells = cells.at[:, :, :, 0].set(0)
    return cells.at[:, :, :, 1].set(CX * CY * CZ - 1)


def draw_live_count(key, part):
    key = jax.random.fold_in(key, 23)
    counts = jax.random.randint(key, (N_GX, N_GY, N_GZ, NB), 1, PTS + 1, dtype=jnp.int32)
    counts = counts.at[:, :, :, 0].set(PTS)
    return counts.at[:, :, :, 1].set(1)


def shard_levels(rng, extent, pieces, low, top_value):
    loudness, own = 1.0, jax.random.fold_in(rng, 6)
    for axis_at, parts in pieces:
        steps = jnp.exp(jax.random.uniform(jax.random.fold_in(own, axis_at), (parts,), jnp.float32, low / len(pieces), top_value / len(pieces)))
        loudness = loudness * jnp.repeat(steps, extent[axis_at] // parts).reshape([-1 if axis == axis_at else 1 for axis in range(len(extent))])
    return loudness


def scatter_about(stream_key, shape, scale, bound, split=(), kind=jnp.bfloat16):
    values = jax.random.normal(stream_key, shape, jnp.float32) * scale
    if len(split) > 0:
        values = shard_levels(stream_key, shape, split, -0.22, 0.18) * values
    return jnp.clip(values, min=-bound, max=bound).astype(kind)


def setup_inputs(seed: int = 0) -> dict:
    key_list = jax.random.split(jax.random.key(seed), 7)
    point_offset = jnp.clip(1.0 * jax.random.uniform(key_list[0], (3, N_GX, N_GY, N_GZ, NB, PTS), jnp.float32) ** shard_levels(key_list[0], (3, N_GX, N_GY, N_GZ, NB, PTS), ((1, 8), (2, 8), (3, 8)), -0.2, 0.2), 0.0, 1.0)
    point_mass = jnp.clip(jnp.exp(math.log(3.0) - 2.3025851 * jax.random.uniform(key_list[1], (N_GX, N_GY, N_GZ, NB, PTS), jnp.float32) ** shard_levels(key_list[1], (N_GX, N_GY, N_GZ, NB, PTS), ((0, 8), (1, 8), (2, 8)), -0.2, 0.2)), 0.3, 3.0)
    point_velocity = scatter_about(key_list[2], (3, N_GX, N_GY, N_GZ, NB, PTS), 1.0, 6.0, ((1, 8), (2, 8), (3, 8)), jnp.float32)
    point_stiffness = jnp.clip(jnp.exp(math.log(2.0) - 2.9957323 * jax.random.uniform(key_list[3], (N_GX, N_GY, N_GZ, NB, PTS), jnp.float32) ** shard_levels(key_list[3], (N_GX, N_GY, N_GZ, NB, PTS), ((0, 8), (1, 8), (2, 8)), -0.2, 0.2)), 0.1, 2.0)
    cell_index = draw_cell_index(jax.random.fold_in(key_list[6], 71), 0)
    live_count = draw_live_count(jax.random.fold_in(key_list[6], 71), 0)
    return dict(point_offset=point_offset, point_mass=point_mass, point_velocity=point_velocity, point_stiffness=point_stiffness, cell_index=cell_index, live_count=live_count)


HIGH = lax.Precision.HIGHEST
BETA = 0.5
GAMMA = 0.3


def corner_weights(frac):
    fx, fy, fz = frac[0], frac[1], frac[2]
    result = []
    for a in range(2):
        for b in range(2):
            for c in range(2):
                wx = fx if a == 1 else 1.0 - fx
                wy = fy if b == 1 else 1.0 - fy
                wz = fz if c == 1 else 1.0 - fz
                result.append(wx * wy * wz)
    return jnp.stack(result)


def offsets():
    found = []
    for dx in (-1, 0, 1):
        for dy in (-1, 0, 1):
            for dz in (-1, 0, 1):
                if dx != 0 or dy != 0 or dz != 0:
                    found.append((dx, dy, dz))
    return found


def make_couplings(stiff):
    found = []
    for dx, dy, dz in offsets():
        coeff = BETA * 0.5 / float(dx * dx + dy * dy + dz * dz)
        near_s = jnp.roll(stiff, (-dx, -dy, -dz), axis=(0, 1, 2))
        found.append((dx, dy, dz, (coeff * (stiff + near_s))[None]))
    return found


def stencil(field, couplings):
    total = jnp.zeros_like(field)
    for dx, dy, dz, weight in couplings:
        near_v = jnp.roll(field, (-dx, -dy, -dz), axis=(1, 2, 3))
        total = total + weight * (field - near_v)
    return total


def reference(point_offset, point_mass, point_velocity, point_stiffness, cell_index, live_count):
    nblk = N_GX * N_GY * N_GZ * NB
    devx = jnp.broadcast_to(jnp.arange(N_GX, dtype=jnp.int32)[:, None, None, None], (N_GX, N_GY, N_GZ, NB)).reshape(nblk)
    devy = jnp.broadcast_to(jnp.arange(N_GY, dtype=jnp.int32)[None, :, None, None], (N_GX, N_GY, N_GZ, NB)).reshape(nblk)
    devz = jnp.broadcast_to(jnp.arange(N_GZ, dtype=jnp.int32)[None, None, :, None], (N_GX, N_GY, N_GZ, NB)).reshape(nblk)
    cells = cell_index.reshape(nblk).astype(jnp.int32)
    cell_i = cells // (CY * CZ)
    cell_j = (cells // CZ) % CY
    cell_k = cells % CZ
    frac = point_offset.reshape(3, nblk, PTS)
    mask = (jnp.arange(PTS, dtype=jnp.int32)[None, :] < live_count.reshape(nblk)[:, None]).astype(jnp.float32)
    mass = point_mass.reshape(nblk, PTS) * mask
    vel = point_velocity.reshape(3, nblk, PTS)
    data = jnp.stack([mass, mass * vel[0], mass * vel[1], mass * vel[2], point_stiffness.reshape(nblk, PTS) * mask])
    wts = corner_weights(frac)
    nodes_all = NX * NY * NZ
    grid = jnp.zeros((nodes_all, 5), jnp.float32)
    node_list = []
    for e in range(8):
        a, b, c = e // 4, (e // 2) % 2, e % 2
        gi = (devx * CX + cell_i + a) % NX
        gj = (devy * CY + cell_j + b) % NY
        gk = (devz * CZ + cell_k + c) % NZ
        node = ((gi * NY + gj) * NZ + gk).astype(jnp.int32)
        node_list.append(node)
        block_sum = jnp.sum(wts[e][None] * data, axis=2)
        grid = grid + jax.ops.segment_sum(block_sum.T, node, num_segments=nodes_all)
    grid = grid.T.reshape(5, NX, NY, NZ)
    total_mass = grid[0] + 1.0
    target = grid[1:4] / total_mass[None]
    stiff = grid[4] + 0.1
    couplings = make_couplings(stiff)
    v = target
    for step in range(NEWTON):
        rhs = -(total_mass[None] * (v - target) + GAMMA * total_mass[None] * v * v * v + stencil(v, couplings))
        diag = total_mass[None] * (1.0 + 3.0 * GAMMA * v * v)
        x = jnp.zeros_like(v)
        r = rhs
        d = rhs
        rr = jnp.sum(r * r)
        for it in range(CG):
            image = diag * d + stencil(d, couplings)
            alpha = rr / jnp.sum(d * image)
            x = x + alpha * d
            r = r - alpha * image
            new_rr = jnp.sum(r * r)
            d = r + (new_rr / rr) * d
            rr = new_rr
        v = v + x
    flat = v.reshape(3, nodes_all)
    out = jnp.zeros((3, nblk, PTS), jnp.float32)
    for e in range(8):
        out = out + wts[e][None] * flat[:, node_list[e]][:, :, None]
    return v, out.reshape(3, N_GX, N_GY, N_GZ, NB, PTS)
```

```python
import functools
import itertools

import jax
import jax.numpy as jnp
from jax import lax
from jax.experimental import pallas as pl
from jax.experimental.pallas import tpu as pltpu
from jax.sharding import PartitionSpec as P

CX = 8
CY = 8
CZ = 128
NB = 128
PTS = 128
N = 8
H = 5
EX = CX + 2 * H
LANES = 2 * CZ
AXES = ("gx", "gy", "gz")
MESH = pl.DeviceIdType.MESH
F32 = jnp.float32
BF16 = jnp.bfloat16
C_ALL = 0.25 * (6.0 + 12.0 / 2.0 + 8.0 / 3.0)
SHIFTS = (0.0, 0.85, 0.45, 0.2)
PEERS = (4, 3, 5, 2, 6, 1, 7)
PAIRS = [(i, j) for i in range(4) for j in range(i, 5)]
NEAR = [o for o in itertools.product((-1, 0, 1), repeat=3) if any(o)]


def slot(o):
    return (o[0] + 1) * 9 + (o[1] + 1) * 3 + (o[2] + 1)


def group(dx, dy):
    return (dx + 1) * 3 + (dy + 1)


REACH = {-1: (0, H + 1), 0: (H, CX + 1), 1: (H + CX, H)}
OWNED = {-1: (0, H), 0: (H, CX), 1: (H + CX, H)}
GIVEN = {-1: 0, 0: 0, 1: CX - H}


def two_sum(a, b):
    s = a + b
    t = s - a
    return s, (a - (s - t)) + (b - t)


def quick_sum(a, b):
    s = a + b
    return s, b - (s - a)


def split(a):
    t = a * 4097.0
    high = t - (t - a)
    return high, a - high


def prod_error(p, a, b):
    return ((a[0] * b[0] - p) + a[0] * b[1] + a[1] * b[0]) + a[1] * b[1]


def pair_add(a, b):
    s, e = two_sum(a[0], b[0])
    return quick_sum(s, e + (a[1] + b[1]))


def pair_mul(a, b):
    p = a[0] * b[0]
    e = prod_error(p, split(a[0]), split(b[0]))
    return quick_sum(p, e + (a[0] * b[1] + a[1] * b[0]))


def pair_div(a, b):
    q = a[0] / b[0]
    qb = pair_mul((q, jnp.zeros_like(q)), b)
    r = pair_add(a, (-qb[0], -qb[1]))
    return quick_sum(q, r[0] / b[0])


def coefficients(gram, hi):
    zero = jnp.zeros_like(gram[0][0])
    g = {}
    for e, (i, j) in enumerate(PAIRS):
        g[i, j] = gram[e]
    d, l = [], {}
    for j in range(4):
        piv = g[j, j]
        floor = jnp.maximum(gram[PAIRS.index((j, j))][0] * 1e-13, 1e-36)
        bad = piv[0] < floor
        piv = (jnp.where(bad, floor, piv[0]), jnp.where(bad, zero, piv[1]))
        d.append(piv)
        for k in range(j + 1, 5):
            l[j, k] = pair_div(g[j, k], piv)
        for i in range(j + 1, 4):
            for k in range(i, 5):
                m = pair_mul(l[j, i], g[j, k])
                g[i, k] = pair_add(g[i, k], (-m[0], -m[1]))
    low = {key: val[0] for key, val in l.items()}
    theta = [hi * s for s in SHIFTS]
    tau = [jnp.ones_like(hi)] + [hi * 0.5] * 3
    a = [theta[0] + tau[0] * low[0, 1]]
    for j in (1, 2, 3):
        a.append(theta[j] + (tau[j] * low[j, j + 1] - tau[j - 1] * low[j - 1, j]))
    ratio = [None] + [d[j][0] / d[j - 1][0] for j in (1, 2, 3)]
    c = [jnp.maximum(a[0], 1.0)]
    for j in (1, 2, 3):
        c.append(jnp.maximum(a[j] - tau[j - 1] * tau[j - 1] * ratio[j] / c[j - 1], 1.0))
    f = [jnp.ones_like(hi)]
    for j in (1, 2, 3):
        f.append(-(tau[j - 1] * f[j - 1]) / c[j - 1])
    z = [None] * 4
    z[3] = f[3] / c[3]
    for j in (2, 1, 0):
        z[j] = (f[j] - tau[j] * ratio[j + 1] * z[j + 1]) / c[j]
    y = [None] * 4
    y[3] = z[3]
    y[2] = z[2] - low[2, 3] * y[3]
    y[1] = z[1] - low[1, 2] * y[2] - low[1, 3] * y[3]
    y[0] = z[0] - low[0, 1] * y[1] - low[0, 2] * y[2] - low[0, 3] * y[3]
    return y


def kernel(off, mass, vel, stiff, cell, live, v_out, u_out,
           tr, rx, kt, am, dep, w_s, v0_s, a1_s, a2_s, mb_s, d_s, e_s, f_s, gs, ns, pk, p4,
           v4, zp, rv, rz, ars, arb, ut, vq, qg,
           dep_ss, dep_rs, v_ss, v_rs, ar_ss, ar_rs):
    me = [lax.axis_index(a) for a in AXES]

    def peer(o):
        return tuple(m if q == 0 else lax.rem(m + (q % N), N) for m, q in zip(me, o))

    greeted = set((o[0] % N, o[1] % N, o[2] % N) for o in NEAR)
    for axis in range(3):
        for q in PEERS:
            greeted.add(tuple(q if i == axis else 0 for i in range(3)))
    barrier = pltpu.get_barrier_semaphore()
    for o in sorted(greeted):
        pl.semaphore_signal(barrier, inc=1, device_id=peer(o), device_id_type=MESH)

    row = lax.broadcasted_iota(jnp.int32, (8, LANES), 0)
    low8 = row < 4
    empty = (row & 3) == 3
    low = lax.broadcasted_iota(jnp.int32, (8, 128), 0) < 4
    lane = lax.broadcasted_iota(jnp.int32, (8, 128), 1)
    rows8 = lax.broadcasted_iota(jnp.int32, (8, 128), 0)

    keep = lax.broadcasted_iota(jnp.int32, (PTS, NB), 0) < live[...]
    for i in range(3):
        tr[i] = off[i].T
        tr[3 + i] = vel[i].T
    tr[6] = jnp.where(keep, stiff[...].T, 0.0)
    tr[7] = jnp.where(keep, mass[...].T, 0.0)

    def sums(i, acc):
        at = pl.ds(pl.multiple_of(i * 8, 8), 8)
        fx, fy, fz = tr[0, at], tr[1, at], tr[2, at]
        m = tr[7, at]
        data = [m * tr[3, at], m * tr[4, at], m * tr[5, at], tr[6, at], m]
        new = []
        for wx in (1.0 - fx, fx):
            for wy in (1.0 - fy, fy):
                wxy = wx * wy
                for wz in (1.0 - fz, fz):
                    wt = wxy * wz
                    for value in data:
                        new.append(acc[len(new)] + wt * value)
        return tuple(new)

    acc = lax.fori_loop(0, PTS // 8, sums, tuple(jnp.zeros((8, NB), F32) for _ in range(40)))
    for e in range(40):
        rx[13, e:e + 1, :] = jnp.sum(acc[e], axis=0, keepdims=True)
    rx[13, 40:41, :] = cell[...].astype(F32)
    rx[13, 41:48, :] = jnp.zeros((7, NB), F32)

    pl.semaphore_wait(barrier, len(greeted))

    def neg(o):
        return tuple(-q for q in o)

    def deposit_copy(o):
        return pltpu.make_async_remote_copy(
            src_ref=rx.at[13], dst_ref=rx.at[slot(neg(o))], send_sem=dep_ss.at[slot(o)],
            recv_sem=dep_rs.at[slot(neg(o))], device_id=peer(o), device_id_type=MESH)

    def v_copy(o):
        if o[2] == 0:
            gx0, gy0 = GIVEN[o[0]], GIVEN[o[1]]
            nx, ny = OWNED[-o[0]][1], OWNED[-o[1]][1]
            src = v4.at[pl.ds(gx0, nx), pl.ds(gy0, ny)]
            dst = rv.at[group(-o[0], -o[1]), pl.ds(0, nx), pl.ds(0, ny)]
        else:
            gx0, nx = GIVEN[o[0]], OWNED[-o[0]][1]
            src = zp.at[pl.ds(gx0, nx)]
            dst = rz.at[group(-o[0], -o[1]), (1 - o[2]) // 2, pl.ds(0, nx)]
        return pltpu.make_async_remote_copy(
            src_ref=src, dst_ref=dst, send_sem=v_ss.at[slot(o)], recv_sem=v_rs.at[slot(neg(o))],
            device_id=peer(o), device_id_type=MESH)

    def ar_start(k, p, value):
        ars[k, p] = value
        for j, q in enumerate(PEERS):
            axis = 2 - p
            pltpu.make_async_remote_copy(
                src_ref=ars.at[k, p], dst_ref=arb.at[k, p, j], send_sem=ar_ss.at[k, p],
                recv_sem=ar_rs.at[k, p], device_id=peer(tuple(q if i == axis else 0 for i in range(3))),
                device_id_type=MESH).start()

    def ar_wait(k, p):
        pltpu.make_async_copy(arb.at[k, p], arb.at[k, p], ar_rs.at[k, p]).wait()

    order = sorted(NEAR, key=lambda o: -sum(abs(q) for q in o))
    for o in order:
        deposit_copy(o).start()

    zrow = lax.broadcasted_iota(jnp.int32, (LANES, NB), 0)
    zrow = jnp.where(zrow >= 192, zrow - LANES, zrow)

    def cells(n):
        c = rx[n, 40:41, :].astype(jnp.int32)
        return c >> 10, (c >> 7) & 7, c & 127

    def add_group(dx, dy, zs):
        (x0, nx), (y0, ny) = REACH[dx], REACH[dy]
        width = 256 * len(zs)
        for zi, dz in enumerate(zs):
            n = slot((dx, dy, dz))
            ci, cj, ck = cells(n)
            for c in range(2):
                at = pl.ds((zi * 2 + c) * 128, 128)
                kt[:, at] = jnp.where(zrow == ck + (c + CZ * dz), 1.0, 0.0).astype(BF16)
                u = {}
                ys = {}
                for b in range(2):
                    for yi in range(ny):
                        hit = cj + (b + 8 * dy + H) == y0 + yi
                        ys[b, yi] = jnp.broadcast_to(jnp.where(hit, 1.0, 0.0), (16, NB)).astype(BF16)
                for a in range(2):
                    s16 = []
                    for b in range(2):
                        e = a * 4 + b * 2 + c
                        s = rx[n, 5 * e:5 * e + 8, :]
                        high = s.astype(BF16).astype(F32)
                        s16.append(jnp.concatenate([high, s - high], axis=0).astype(BF16))
                    for yi in range(ny):
                        u[a, yi] = ys[0, yi] * s16[0] + ys[1, yi] * s16[1]

                def plane(xi, _):
                    xs = []
                    for a in range(2):
                        hit = ci + (a + 8 * dx + H) == x0 + xi
                        xs.append(jnp.broadcast_to(jnp.where(hit, 1.0, 0.0), (16, NB)).astype(BF16))
                    for yi in range(ny):
                        am[xi * ny + yi, :, at] = xs[0] * u[0, yi] + xs[1] * u[1, yi]
                    return 0

                lax.fori_loop(0, nx, plane, 0)
        lhs = am[0:nx * ny, :, 0:width].reshape(nx * ny * 16, width)
        out = lax.dot_general(lhs, kt[:, 0:width], (((1,), (1,)), ((), ())), preferred_element_type=F32)
        out = out.reshape(nx, ny, 16, LANES)
        dep[x0:x0 + nx, y0:y0 + ny] += out[:, :, 0:8] + out[:, :, 8:16]

    def clear(x, _):
        dep[x] = jnp.zeros((EX, 8, LANES), F32)
        return 0

    lax.fori_loop(0, EX, clear, 0)
    add_group(0, 0, (0,))

    def node(x, y):
        t = dep[x, y]
        mb = jnp.broadcast_to(dep[x, y, 4:5, :], (8, LANES)) + 1.0
        sb = jnp.broadcast_to(dep[x, y, 3:4, :], (8, LANES)) + 0.1
        dup = jnp.where(low8, t, pltpu.roll(t, 4, 0))
        return jnp.where(empty, 0.0, dup / mb), mb, sb

    def estimate(x, best):
        for y in range(H, H + CY + 1):
            v, mb, sb = node(x, y)
            vv = v * v
            damped = v * (1.0 + 0.6 * vv) / (1.0 + 0.9 * vv)
            vv = jnp.where(low8, vv, damped * damped)
            best = jnp.maximum(best, mb * (1.0 + 0.9 * vv) + 5.0 * sb)
        return best

    best = lax.fori_loop(H, H + CX + 1, estimate, jnp.zeros((8, LANES), F32))
    best = jnp.maximum(best[:, 0:128], best[:, 128:256])
    ar_start(0, 0, best)

    def wait_group(dx, dy):
        for dz in (-1, 0, 1):
            if (dx, dy, dz) != (0, 0, 0):
                deposit_copy((-dx, -dy, -dz)).wait_recv()

    def ar_max(k, p, best):
        ar_wait(k, p)
        for j in range(7):
            best = jnp.maximum(best, arb[k, p, j])
        return best

    wait_group(0, 0)
    add_group(0, 0, (-1, 1))
    best = ar_max(0, 0, best)
    ar_start(0, 1, best)
    groups = [(-1, 0), (1, 0), (0, -1), (0, 1), (-1, -1), (-1, 1), (1, -1), (1, 1)]
    for i, (dx, dy) in enumerate(groups):
        wait_group(dx, dy)
        add_group(dx, dy, (-1, 0, 1))
        if i == 2:
            best = ar_max(0, 1, best)
            ar_start(0, 2, best)

    def coefs(x, _):
        for y in range(EX):
            v, mb, sb = node(x, y)
            a2 = jnp.where(low8, 0.125, 0.125 * sb)
            w_s[x, y] = v
            mb_s[x, y] = mb
            a1_s[x, y] = jnp.where(low8, sb, 1.0)
            a2_s[x, y] = a2
            d_s[x, y] = C_ALL * sb
            f_s[x, y] = jnp.where(row == 3, 0.125 * sb, a2 * v)
        return 0

    lax.fori_loop(0, EX, coefs, 0)

    def level(k, emit):
        first, last = H - k, H + CX + k
        wide = LANES if k else CZ

        def sweep(x, _):
            h = {}
            for y in range(first - 1, last + 1):
                f = f_s[x, y]
                sz = pltpu.roll(f, 1, 1) + pltpu.roll(f, LANES - 1, 1)
                f, sz = f[:, 0:wide], sz[:, 0:wide]
                h[y] = (sz + sz, f + f + sz, f + (2.0 / 3.0) * sz)
                if y - 2 >= first - 1:
                    m = y - 1
                    gs[x, m, :, 0:wide] = h[m][1] + (h[m - 1][2] + h[m + 1][2])
                    ns[x, m, :, 0:wide] = h[m][0] + (h[m - 1][1] + h[m + 1][1])
            return 0

        lax.fori_loop(first - 1, last + 1, sweep, 0)

        def combine(x, _):
            for y in range(first, last):
                emit(x, y, ns[x, y, :, 0:wide] + (gs[x - 1, y, :, 0:wide] + gs[x + 1, y, :, 0:wide]))
            return 0

        lax.fori_loop(first, last, combine, 0)

    def folded(x, y, sums, wide):
        q = a1_s[x, y, :, 0:wide] * sums
        return q + pltpu.roll(q, 4, 0)

    def first_residual(x, y, sums):
        d = d_s[x, y] + jnp.broadcast_to(sums[3:4, :], (8, LANES))
        d_s[x, y] = d
        lq = folded(x, y, sums, LANES)
        v = w_s[x, y]
        mb = mb_s[x, y]
        mvv = mb * v * v
        e_s[x, y] = mb + 0.9 * mvv + d
        p = jnp.where(empty, 0.0, lq - (d + 0.3 * mvv) * v)
        pk[0, x, y] = p
        f_s[x, y] = a2_s[x, y] * p

    def second_residual(x, y, sums):
        d = d_s[x, y]
        lq = folded(x, y, sums, LANES)
        v = w_s[x, y]
        mb = mb_s[x, y]
        mvv = mb * v * v
        e_s[x, y] = mb + 0.9 * mvv + d
        p = lq - (d + 0.3 * mvv) * v - mb * (v - v0_s[x, y])
        pk[0, x, y] = p
        f_s[x, y] = a2_s[x, y] * p

    def basis(k, hi):
        theta = hi * SHIFTS[k]
        inv = 2.0 / hi
        wide = CZ if k == 3 else LANES
        theta = jnp.broadcast_to(theta, (8, wide))
        inv = jnp.broadcast_to(inv, (8, wide))

        def emit(x, y, sums):
            lq = folded(x, y, sums, wide)
            e = e_s[x, y, :, 0:wide]
            if k:
                e = e - theta
            p = e * pk[k, x, y, :, 0:wide] - lq
            if k:
                p = p * inv
            if k == 3:
                p4[x - H, y - H] = p
            else:
                pk[k + 1, x, y] = p
                f_s[x, y] = a2_s[x, y] * p

        level(3 - k, emit)

    def gram():
        def plane(x, carry):
            acc = list(carry)
            for y in range(4):
                p = [jnp.where(low, pk[i, H + x, H + y, :, 0:128], pk[i, H + x, H + 4 + y, :, 0:128]) for i in range(4)]
                p.append(jnp.where(low, p4[x, y], p4[x, y + 4]))
                parts = [split(q) for q in p]
                for e, (i, j) in enumerate(PAIRS):
                    m = p[i] * p[j]
                    err = prod_error(m, parts[i], parts[j])
                    s, t = two_sum(acc[2 * e], m)
                    acc[2 * e] = s
                    acc[2 * e + 1] = acc[2 * e + 1] + (t + err)
            return tuple(acc)

        acc = lax.fori_loop(0, CX, plane, tuple(jnp.zeros((8, 128), F32) for _ in range(28)))
        packed = []
        for part in range(2):
            high = jnp.zeros((8, 128), F32)
            rest = jnp.zeros((8, 128), F32)
            for r in range(8):
                e = part * 8 + r
                if e >= 14:
                    continue
                a = (acc[2 * e], acc[2 * e + 1])
                for s in (4, 2, 1):
                    a = pair_add(a, (pltpu.roll(a[0], s, 0), pltpu.roll(a[1], s, 0)))
                high = jnp.where(rows8 == r, a[0], high)
                rest = jnp.where(rows8 == r, a[1], rest)
            a = (high, rest)
            for s in (64, 32, 16, 8, 4, 2, 1):
                a = pair_add(a, (pltpu.roll(a[0], s, 1), pltpu.roll(a[1], s, 1)))
            packed.append(a)
        return jnp.where(lane < 32, packed[0][0], jnp.where(lane < 64, packed[0][1], jnp.where(lane < 96, packed[1][0], packed[1][1])))

    even = (lane & 32) == 0

    def ar_sum(k, p, own):
        ar_wait(k, p)
        total = (own, pltpu.roll(own, 96, 1))
        for j in range(7):
            other = arb[k, p, j]
            total = pair_add(total, (other, pltpu.roll(other, 96, 1)))
        return jnp.where(even, total[0], pltpu.roll(total[1], 32, 1))

    def solve(k, hi):
        g = gram()
        for p in range(3):
            ar_start(k, p, g)
            g = ar_sum(k, p, g)
        entries = []
        for e in range(14):
            r, base = e % 8, 64 * (e // 8)
            entries.append(tuple(jnp.broadcast_to(g[r:r + 1, base + s:base + s + 1], (8, 128)) for s in (0, 32)))
        return coefficients(entries, hi)

    first_hi = None
    level(4, first_residual)
    basis(0, jnp.ones((1, 1), F32))
    best = ar_max(0, 2, best)
    hi1 = jnp.max(jnp.max(jnp.where(low, best, 0.0), axis=0, keepdims=True), axis=1, keepdims=True)
    hi2 = jnp.max(jnp.max(jnp.where(low, 0.0, best), axis=0, keepdims=True), axis=1, keepdims=True)
    for k in (1, 2, 3):
        basis(k, hi1)
    y1 = solve(1, jnp.broadcast_to(hi1, (8, 128)))

    slots = [(lane >= 16 * y - 5) & (lane < 16 * y + 5) for y in range(8)]
    slots[0] = (lane < 5) | (lane >= 123)

    def update(x, _):
        packed = jnp.zeros((8, 128), F32)
        for y in range(CY):
            v = w_s[H + x, H + y, :, 0:128]
            for i in range(4):
                v = v + y1[i] * pk[i, H + x, H + y, :, 0:128]
            v4[x, y] = v[0:4, :]
            w_s[H + x, H + y, :, 0:128] = v
            packed = jnp.where(slots[y], pltpu.roll(v, (16 * y) % 128, 1) if y else v, packed)
        zp[x] = packed[0:4, :]
        return 0

    def keep_target(x, _):
        for y in range(1, EX - 1):
            v0_s[x, y] = w_s[x, y]
        return 0

    lax.fori_loop(1, EX - 1, keep_target, 0)
    lax.fori_loop(0, CX, update, 0)
    for o in order:
        v_copy(o).start()

    near_low = (lane & 15) < 8

    def take(dx, dy):
        (x0, nx), (y0, ny) = OWNED[dx], OWNED[dy]
        gy0 = GIVEN[-dy]
        g = group(dx, dy)
        for dz in (-1, 0, 1):
            if (dx, dy, dz) != (0, 0, 0):
                v_copy((-dx, -dy, -dz)).wait_recv()

        def plane(x, _):
            after = rz[g, 1, x]
            before = rz[g, 0, x]
            after = jnp.concatenate([after, after], axis=0)
            before = jnp.concatenate([before, before], axis=0)
            ends = jnp.where(near_low, after, before)
            for y in range(ny):
                sy = (128 - 16 * (gy0 + y)) % 128
                tail = pltpu.roll(ends, sy, 1) if sy else ends
                w_s[x0 + x, y0 + y, :, 128:256] = tail
                f_s[x0 + x, y0 + y, :, 128:256] = a2_s[x0 + x, y0 + y, :, 128:256] * tail
                if (dx, dy) == (0, 0):
                    head = w_s[x0 + x, y0 + y, :, 0:128]
                else:
                    head = rv[g, x, y]
                    head = jnp.concatenate([head, head], axis=0)
                    w_s[x0 + x, y0 + y, :, 0:128] = head
                f_s[x0 + x, y0 + y, :, 0:128] = a2_s[x0 + x, y0 + y, :, 0:128] * head
            return 0

        lax.fori_loop(0, nx, plane, 0)

    take(0, 0)
    for dx, dy in groups:
        take(dx, dy)

    level(4, second_residual)
    for k in range(4):
        basis(k, hi2)
    y2 = solve(2, jnp.broadcast_to(hi2, (8, 128)))
    y2 = [jnp.concatenate([q, q], axis=1) for q in y2]

    def finish(x, _):
        for y in range(CY + 1):
            v = w_s[H + x, H + y]
            for i in range(4):
                v = v + y2[i] * pk[i, H + x, H + y]
            w_s[H + x, H + y] = v
            high = v.astype(BF16).astype(F32)
            vq[x * 9 + y] = jnp.where(low8, high, v - high)
        return 0

    lax.fori_loop(0, CX + 1, finish, 0)
    for f in range(3):
        for x in range(CX):
            for y in range(CY):
                v_out[f, x, y:y + 1, :] = w_s[H + x, H + y, f:f + 1, 0:128]

    ci, cj, ck = cells(13)
    for c in range(2):
        kt[:, c * 128:(c + 1) * 128] = jnp.where(zrow == ck + c, 1.0, 0.0).astype(BF16)
    qg[...] = jnp.dot(vq[...].reshape(81 * 8, LANES).astype(BF16), kt[:, 0:256],
                      preferred_element_type=F32).reshape(81, 8, LANES)
    ci = jnp.broadcast_to(jnp.concatenate([ci, ci], axis=1), (8, LANES))
    cj = jnp.broadcast_to(jnp.concatenate([cj, cj], axis=1), (8, LANES))
    corner = {}
    for a in range(2):
        at_x = []
        for y in range(9):
            z = qg[a * 9 + y]
            for x in range(1, 8):
                z = jnp.where(ci == x, qg[(x + a) * 9 + y], z)
            at_x.append(z)
        for b in range(2):
            z = at_x[b]
            for y in range(1, 8):
                z = jnp.where(cj == y, at_x[y + b], z)
            corner[a, b] = z + pltpu.roll(z, 4, 0)

    def points(i, _):
        at = pl.ds(pl.multiple_of(i * 8, 8), 8)
        fx, fy, fz = tr[0, at], tr[1, at], tr[2, at]
        gx, gy, gz = 1.0 - fx, 1.0 - fy, 1.0 - fz
        w = {(0, 0): gx * gy, (0, 1): gx * fy, (1, 0): fx * gy, (1, 1): fx * fy}
        for f in range(3):
            total = None
            for key, wt in w.items():
                r = corner[key]
                term = wt * (gz * r[f:f + 1, 0:128] + fz * r[f:f + 1, 128:256])
                total = term if total is None else total + term
            ut[f, at] = total
        return 0

    lax.fori_loop(0, PTS // 8, points, 0)
    for f in range(3):
        u_out[f] = ut[f].T

    for o in order:
        deposit_copy(o).wait_send()
        v_copy(o).wait_send()
    for k in range(3):
        for p in range(3):
            pltpu.make_async_copy(arb.at[k, p], arb.at[k, p], ar_ss.at[k, p]).wait()


def shards(point_offset, point_mass, point_velocity, point_stiffness, cell_index, live_count):
    vm = pl.BlockSpec(memory_space=pltpu.VMEM)
    ext = pltpu.VMEM((EX, EX, 8, LANES), F32)
    v, u = pl.pallas_call(
        kernel,
        out_shape=(jax.ShapeDtypeStruct((3, CX, CY, CZ), F32), jax.ShapeDtypeStruct((3, NB, PTS), F32)),
        in_specs=[vm] * 6,
        out_specs=(vm, vm),
        scratch_shapes=[
            pltpu.VMEM((8, PTS, NB), F32),
            pltpu.VMEM((27, 48, NB), F32),
            pltpu.VMEM((LANES, 768), BF16),
            pltpu.VMEM((81, 16, 768), BF16),
            ext, ext, ext, ext, ext, ext, ext, ext, ext, ext, ext,
            pltpu.VMEM((4, EX, EX, 8, LANES), F32),
            pltpu.VMEM((CX, CY, 8, CZ), F32),
            pltpu.VMEM((CX, CY, 4, CZ), F32),
            pltpu.VMEM((CX, 4, CZ), F32),
            pltpu.VMEM((9, CX, CY, 4, CZ), F32),
            pltpu.VMEM((9, 2, CX, 4, CZ), F32),
            pltpu.VMEM((3, 3, 8, 128), F32),
            pltpu.VMEM((3, 3, 7, 8, 128), F32),
            pltpu.VMEM((3, PTS, NB), F32),
            pltpu.VMEM((81, 8, LANES), F32),
            pltpu.VMEM((81, 8, LANES), F32),
            pltpu.SemaphoreType.DMA((27,)),
            pltpu.SemaphoreType.DMA((27,)),
            pltpu.SemaphoreType.DMA((27,)),
            pltpu.SemaphoreType.DMA((27,)),
            pltpu.SemaphoreType.DMA((3, 3)),
            pltpu.SemaphoreType.DMA((3, 3)),
        ],
        compiler_params=pltpu.CompilerParams(
            collective_id=0, has_side_effects=True, vmem_limit_bytes=60 << 20),
        name="granular_step",
    )(
        point_offset.reshape(3, NB, PTS),
        point_mass.reshape(NB, PTS),
        point_velocity.reshape(3, NB, PTS),
        point_stiffness.reshape(NB, PTS),
        cell_index.reshape(1, NB),
        live_count.reshape(1, NB),
    )
    return v, u.reshape(3, 1, 1, 1, NB, PTS)


def solution(mesh):
    return jax.shard_map(
        shards,
        mesh=mesh,
        in_specs=(
            P(None, "gx", "gy", "gz", None, None),
            P("gx", "gy", "gz", None, None),
            P(None, "gx", "gy", "gz", None, None),
            P("gx", "gy", "gz", None, None),
            P("gx", "gy", "gz", None),
            P("gx", "gy", "gz", None),
        ),
        out_specs=(P(None, "gx", "gy", "gz"), P(None, "gx", "gy", "gz", None, None)),
        check_vma=False,
    )
```

```python
import functools
import itertools

import jax
import jax.numpy as jnp
from jax import lax
from jax.experimental import pallas as pl
from jax.experimental.pallas import tpu as pltpu
from jax.sharding import PartitionSpec as P

CX = 8
CY = 8
CZ = 128
NB = 128
PTS = 128
N = 8
H = 5
EX = CX + 2 * H
LANES = 2 * CZ
AXES = ("gx", "gy", "gz")
MESH = pl.DeviceIdType.MESH
F32 = jnp.float32
BF16 = jnp.bfloat16
C_ALL = 0.25 * (6.0 + 12.0 / 2.0 + 8.0 / 3.0)
SHIFTS = (0.0, 0.85, 0.45, 0.2)
PEERS = (4, 3, 5, 2, 6, 1, 7)
PAIRS = [(i, j) for i in range(4) for j in range(i, 5)]
NEAR = [o for o in itertools.product((-1, 0, 1), repeat=3) if any(o)]


def slot(o):
    return (o[0] + 1) * 9 + (o[1] + 1) * 3 + (o[2] + 1)


def group(dx, dy):
    return (dx + 1) * 3 + (dy + 1)


REACH = {-1: (0, H + 1), 0: (H, CX + 1), 1: (H + CX, H)}
OWNED = {-1: (0, H), 0: (H, CX), 1: (H + CX, H)}
GIVEN = {-1: 0, 0: 0, 1: CX - H}


def two_sum(a, b):
    s = a + b
    t = s - a
    return s, (a - (s - t)) + (b - t)


def quick_sum(a, b):
    s = a + b
    return s, b - (s - a)


def split(a):
    t = a * 4097.0
    high = t - (t - a)
    return high, a - high


def prod_error(p, a, b):
    return ((a[0] * b[0] - p) + a[0] * b[1] + a[1] * b[0]) + a[1] * b[1]


def pair_add(a, b):
    s, e = two_sum(a[0], b[0])
    return quick_sum(s, e + (a[1] + b[1]))


def pair_mul(a, b):
    p = a[0] * b[0]
    e = prod_error(p, split(a[0]), split(b[0]))
    return quick_sum(p, e + (a[0] * b[1] + a[1] * b[0]))


def pair_div(a, b):
    q = a[0] / b[0]
    qb = pair_mul((q, jnp.zeros_like(q)), b)
    r = pair_add(a, (-qb[0], -qb[1]))
    return quick_sum(q, r[0] / b[0])


def coefficients(gram, hi):
    zero = jnp.zeros_like(gram[0][0])
    g = {}
    for e, (i, j) in enumerate(PAIRS):
        g[i, j] = gram[e]
    d, l = [], {}
    for j in range(4):
        piv = g[j, j]
        floor = jnp.maximum(gram[PAIRS.index((j, j))][0] * 1e-13, 1e-36)
        bad = piv[0] < floor
        piv = (jnp.where(bad, floor, piv[0]), jnp.where(bad, zero, piv[1]))
        d.append(piv)
        for k in range(j + 1, 5):
            l[j, k] = pair_div(g[j, k], piv)
        for i in range(j + 1, 4):
            for k in range(i, 5):
                m = pair_mul(l[j, i], g[j, k])
                g[i, k] = pair_add(g[i, k], (-m[0], -m[1]))
    low = {key: val[0] for key, val in l.items()}
    theta = [hi * s for s in SHIFTS]
    tau = [jnp.ones_like(hi)] + [hi * 0.5] * 3
    a = [theta[0] + tau[0] * low[0, 1]]
    for j in (1, 2, 3):
        a.append(theta[j] + (tau[j] * low[j, j + 1] - tau[j - 1] * low[j - 1, j]))
    ratio = [None] + [d[j][0] / d[j - 1][0] for j in (1, 2, 3)]
    c = [jnp.maximum(a[0], 1.0)]
    for j in (1, 2, 3):
        c.append(jnp.maximum(a[j] - tau[j - 1] * tau[j - 1] * ratio[j] / c[j - 1], 1.0))
    f = [jnp.ones_like(hi)]
    for j in (1, 2, 3):
        f.append(-(tau[j - 1] * f[j - 1]) / c[j - 1])
    z = [None] * 4
    z[3] = f[3] / c[3]
    for j in (2, 1, 0):
        z[j] = (f[j] - tau[j] * ratio[j + 1] * z[j + 1]) / c[j]
    y = [None] * 4
    y[3] = z[3]
    y[2] = z[2] - low[2, 3] * y[3]
    y[1] = z[1] - low[1, 2] * y[2] - low[1, 3] * y[3]
    y[0] = z[0] - low[0, 1] * y[1] - low[0, 2] * y[2] - low[0, 3] * y[3]
    return y


def kernel(off, mass, vel, stiff, cell, live, v_out, u_out,
           tr, rx, kt0, kt1, am0, am1, dep, w_s, v0_s, a1_s, a2_s, mb_s, d_s, e_s, f_s, gs, ns, pk, p4,
           v4, zp, rv, rz, ars, arb, ut, vq, qg,
           dep_ss, dep_rs, v_ss, v_rs, ar_ss, ar_rs):
    me = [lax.axis_index(a) for a in AXES]
    kts, ams = (kt0, kt1), (am0, am1)

    def peer(o):
        return tuple(m if q == 0 else lax.rem(m + (q % N), N) for m, q in zip(me, o))

    greeted = set((o[0] % N, o[1] % N, o[2] % N) for o in NEAR)
    for axis in range(3):
        for q in PEERS:
            greeted.add(tuple(q if i == axis else 0 for i in range(3)))
    barrier = pltpu.get_barrier_semaphore()
    for o in sorted(greeted):
        pl.semaphore_signal(barrier, inc=1, device_id=peer(o), device_id_type=MESH)

    row = lax.broadcasted_iota(jnp.int32, (8, LANES), 0)
    low8 = row < 4
    empty = (row & 3) == 3
    low = lax.broadcasted_iota(jnp.int32, (8, 128), 0) < 4
    lane = lax.broadcasted_iota(jnp.int32, (8, 128), 1)
    rows8 = lax.broadcasted_iota(jnp.int32, (8, 128), 0)

    keep = lax.broadcasted_iota(jnp.int32, (PTS, NB), 0) < live[...]
    for i in range(3):
        tr[i] = off[i].T
        tr[3 + i] = vel[i].T
    tr[6] = jnp.where(keep, stiff[...].T, 0.0)
    tr[7] = jnp.where(keep, mass[...].T, 0.0)

    def sums(i, acc):
        at = pl.ds(pl.multiple_of(i * 8, 8), 8)
        fx, fy, fz = tr[0, at], tr[1, at], tr[2, at]
        m = tr[7, at]
        data = [m * tr[3, at], m * tr[4, at], m * tr[5, at], tr[6, at], m]
        new = []
        for wx in (1.0 - fx, fx):
            for wy in (1.0 - fy, fy):
                wxy = wx * wy
                for wz in (1.0 - fz, fz):
                    wt = wxy * wz
                    for value in data:
                        new.append(acc[len(new)] + wt * value)
        return tuple(new)

    acc = lax.fori_loop(0, PTS // 8, sums, tuple(jnp.zeros((8, NB), F32) for _ in range(40)))
    for e in range(40):
        rx[13, e:e + 1, :] = jnp.sum(acc[e], axis=0, keepdims=True)
    rx[13, 40:41, :] = cell[...].astype(F32)
    rx[13, 41:48, :] = jnp.zeros((7, NB), F32)

    pl.semaphore_wait(barrier, len(greeted))

    def neg(o):
        return tuple(-q for q in o)

    def deposit_copy(o):
        return pltpu.make_async_remote_copy(
            src_ref=rx.at[13], dst_ref=rx.at[slot(neg(o))], send_sem=dep_ss.at[slot(o)],
            recv_sem=dep_rs.at[slot(neg(o))], device_id=peer(o), device_id_type=MESH)

    def v_copy(o):
        if o[2] == 0:
            gx0, gy0 = GIVEN[o[0]], GIVEN[o[1]]
            nx, ny = OWNED[-o[0]][1], OWNED[-o[1]][1]
            src = v4.at[pl.ds(gx0, nx), pl.ds(gy0, ny)]
            dst = rv.at[group(-o[0], -o[1]), pl.ds(0, nx), pl.ds(0, ny)]
        else:
            gx0, nx = GIVEN[o[0]], OWNED[-o[0]][1]
            src = zp.at[pl.ds(gx0, nx)]
            dst = rz.at[group(-o[0], -o[1]), (1 - o[2]) // 2, pl.ds(0, nx)]
        return pltpu.make_async_remote_copy(
            src_ref=src, dst_ref=dst, send_sem=v_ss.at[slot(o)], recv_sem=v_rs.at[slot(neg(o))],
            device_id=peer(o), device_id_type=MESH)

    def ar_start(k, p, value):
        ars[k, p, 0:8] = value[0]
        ars[k, p, 8:16] = value[1]
        for j, q in enumerate(PEERS):
            axis = 2 - p
            pltpu.make_async_remote_copy(
                src_ref=ars.at[k, p], dst_ref=arb.at[k, p, j], send_sem=ar_ss.at[k, p],
                recv_sem=ar_rs.at[k, p], device_id=peer(tuple(q if i == axis else 0 for i in range(3))),
                device_id_type=MESH).start()

    def ar_wait(k, p):
        pltpu.make_async_copy(arb.at[k, p], arb.at[k, p], ar_rs.at[k, p]).wait()

    order = sorted(NEAR, key=lambda o: -sum(abs(q) for q in o))
    for o in order:
        deposit_copy(o).start()

    zrow = lax.broadcasted_iota(jnp.int32, (LANES, NB), 0)
    zrow = jnp.where(zrow >= 192, zrow - LANES, zrow)

    def cells(n):
        c = rx[n, 40:41, :].astype(jnp.int32)
        return c >> 10, (c >> 7) & 7, c & 127

    def add_group(dx, dy, zs, which):
        kt, am = kts[which], ams[which]
        (x0, nx), (y0, ny) = REACH[dx], REACH[dy]
        width = 256 * len(zs)
        for zi, dz in enumerate(zs):
            n = slot((dx, dy, dz))
            ci, cj, ck = cells(n)
            for c in range(2):
                at = pl.ds((zi * 2 + c) * 128, 128)
                kt[:, at] = jnp.where(zrow == ck + (c + CZ * dz), 1.0, 0.0).astype(BF16)
                ys, xs = [], []
                for b in range(2):
                    plane = lax.broadcasted_iota(jnp.int32, (ny, 16, NB), 0)
                    ys.append(jnp.where(plane == cj + (b + 8 * dy + H - y0), 1.0, 0.0).astype(BF16))
                    plane = lax.broadcasted_iota(jnp.int32, (nx, 16, NB), 0)
                    xs.append(jnp.where(plane == ci + (b + 8 * dx + H - x0), 1.0, 0.0).astype(BF16))
                total = None
                for a in range(2):
                    u = None
                    for b in range(2):
                        e = a * 4 + b * 2 + c
                        s = rx[n, 5 * e:5 * e + 8, :]
                        high = s.astype(BF16).astype(F32)
                        s16 = jnp.concatenate([high, s - high], axis=0).astype(BF16)
                        term = ys[b] * s16
                        u = term if u is None else u + term
                    term = xs[a].reshape(nx, 1, 16, NB) * u.reshape(1, ny, 16, NB)
                    total = term if total is None else total + term
                am[0:nx * ny, :, at] = total.reshape(nx * ny, 16, NB)
        lhs = am[0:nx * ny, :, 0:width].reshape(nx * ny * 16, width)
        out = lax.dot_general(lhs, kt[:, 0:width], (((1,), (1,)), ((), ())), preferred_element_type=F32)
        out = out.reshape(nx, ny, 16, LANES)
        dep[x0:x0 + nx, y0:y0 + ny] += out[:, :, 0:8] + out[:, :, 8:16]

    dep[...] = jnp.zeros((EX, EX, 8, LANES), F32)
    add_group(0, 0, (0,), 1)

    def node(x, ys):
        t = dep[x, ys]
        mb = jnp.broadcast_to(dep[x, ys, 4:5, :], t.shape) + 1.0
        sb = jnp.broadcast_to(dep[x, ys, 3:4, :], t.shape) + 0.1
        dup = jnp.where(low8, t, pltpu.roll(t, 4, 1))
        return jnp.where(empty, 0.0, dup / mb), mb, sb

    def estimate(x, best):
        v, mb, sb = node(x, pl.ds(H, CY + 1))
        vv = v * v
        damped = v * (1.0 + 0.6 * vv) / (1.0 + 0.9 * vv)
        vv = jnp.where(low8, vv, damped * damped)
        return jnp.maximum(best, jnp.max(mb * (1.0 + 0.9 * vv) + 5.0 * sb, axis=0))

    best = lax.fori_loop(H, H + CX + 1, estimate, jnp.zeros((8, LANES), F32))
    best = jnp.maximum(best[:, 0:128], best[:, 128:256])
    ar_start(0, 0, (best, best))

    def wait_group(dx, dy):
        for dz in (-1, 0, 1):
            if (dx, dy, dz) != (0, 0, 0):
                deposit_copy((-dx, -dy, -dz)).wait_recv()

    def ar_max(k, p, best):
        ar_wait(k, p)
        for j in range(7):
            best = jnp.maximum(best, arb[k, p, j, 0:8])
        return best

    best = ar_max(0, 0, best)
    ar_start(0, 1, (best, best))
    wait_group(0, 0)
    add_group(0, 0, (-1, 1), 0)
    groups = [(-1, 0), (1, 0), (0, -1), (0, 1), (-1, -1), (-1, 1), (1, -1), (1, 1)]
    for i, (dx, dy) in enumerate(groups):
        wait_group(dx, dy)
        add_group(dx, dy, (-1, 0, 1), (i + 1) % 2)
        if i == 4:
            best = ar_max(0, 1, best)
            ar_start(0, 2, (best, best))

    def coefs(x, _):
        v, mb, sb = node(x, pl.ds(0, EX))
        a2 = jnp.where(low8, 0.125, 0.125 * sb)
        w_s[x] = v
        mb_s[x] = mb
        a1_s[x] = jnp.where(low8, sb, 1.0)
        a2_s[x] = a2
        d_s[x] = C_ALL * sb
        f_s[x] = jnp.where(row == 3, 0.125 * sb, a2 * v)
        return 0

    lax.fori_loop(0, EX, coefs, 0)

    def level(k, emit):
        first, last = H - k, H + CX + k
        ys = pl.ds(first, last - first)
        wide = pl.ds(0, LANES if k else CZ)
        for x in range(first - 1, last + 1):
            f = f_s[x, first - 1:last + 1]
            sz = pltpu.roll(f, 1, 2) + pltpu.roll(f, LANES - 1, 2)
            if not k:
                f, sz = f[:, :, 0:CZ], sz[:, :, 0:CZ]
            h0, h1, h2 = sz + sz, f + f + sz, f + (2.0 / 3.0) * sz
            gs[x, ys, :, wide] = h1[1:-1] + (h2[:-2] + h2[2:])
            ns[x, ys, :, wide] = h0[1:-1] + (h1[:-2] + h1[2:])
        for x in range(first, last):
            emit(x, ys, ns[x, ys, :, wide] + (gs[x - 1, ys, :, wide] + gs[x + 1, ys, :, wide]))

    def folded(x, ys, sums, wide):
        q = a1_s[x, ys, :, wide] * sums
        return q + pltpu.roll(q, 4, 1)

    full = pl.ds(0, LANES)

    def first_residual(x, ys, sums):
        d = d_s[x, ys] + jnp.broadcast_to(sums[:, 3:4, :], sums.shape)
        d_s[x, ys] = d
        lq = folded(x, ys, sums, full)
        v = w_s[x, ys]
        mb = mb_s[x, ys]
        mvv = mb * v * v
        e_s[x, ys] = mb + 0.9 * mvv + d
        p = jnp.where(empty, 0.0, lq - (d + 0.3 * mvv) * v)
        pk[0, x, ys] = p
        f_s[x, ys] = a2_s[x, ys] * p

    def second_residual(x, ys, sums):
        d = d_s[x, ys]
        lq = folded(x, ys, sums, full)
        v = w_s[x, ys]
        mb = mb_s[x, ys]
        mvv = mb * v * v
        e_s[x, ys] = mb + 0.9 * mvv + d
        p = lq - (d + 0.3 * mvv) * v - mb * (v - v0_s[x, ys])
        pk[0, x, ys] = p
        f_s[x, ys] = a2_s[x, ys] * p

    def basis(k, hi):
        lanes = CZ if k == 3 else LANES
        wide = pl.ds(0, lanes)
        theta = jnp.broadcast_to(hi * SHIFTS[k], (8, lanes))
        inv = jnp.broadcast_to(2.0 / hi, (8, lanes))

        def emit(x, ys, sums):
            lq = folded(x, ys, sums, wide)
            e = e_s[x, ys, :, wide]
            if k:
                e = e - theta
            p = e * pk[k, x, ys, :, wide] - lq
            if k:
                p = p * inv
            if k == 3:
                p4[x - H] = p
            else:
                pk[k + 1, x, ys] = p
                f_s[x, ys] = a2_s[x, ys] * p

        level(3 - k, emit)

    def gram():
        def plane(x, carry):
            acc = list(carry)
            for y in range(4):
                p = [jnp.where(low, pk[i, H + x, H + y, :, 0:128], pk[i, H + x, H + 4 + y, :, 0:128]) for i in range(4)]
                p.append(jnp.where(low, p4[x, y], p4[x, y + 4]))
                parts = [split(q) for q in p]
                for e, (i, j) in enumerate(PAIRS):
                    m = p[i] * p[j]
                    err = prod_error(m, parts[i], parts[j])
                    s, t = two_sum(acc[2 * e], m)
                    acc[2 * e] = s
                    acc[2 * e + 1] = acc[2 * e + 1] + (t + err)
            return tuple(acc)

        acc = lax.fori_loop(0, CX, plane, tuple(jnp.zeros((8, 128), F32) for _ in range(28)), unroll=2)
        packed = []
        for part in range(2):
            high = jnp.zeros((8, 128), F32)
            rest = jnp.zeros((8, 128), F32)
            for r in range(8):
                e = part * 8 + r
                if e >= 14:
                    continue
                a = (acc[2 * e], acc[2 * e + 1])
                for s in (4, 2, 1):
                    a = pair_add(a, (pltpu.roll(a[0], s, 0), pltpu.roll(a[1], s, 0)))
                high = jnp.where(rows8 == r, a[0], high)
                rest = jnp.where(rows8 == r, a[1], rest)
            a = (high, rest)
            for s in (64, 32, 16, 8, 4, 2, 1):
                a = pair_add(a, (pltpu.roll(a[0], s, 1), pltpu.roll(a[1], s, 1)))
            packed.append(a)
        return tuple(jnp.where(lane < 64, packed[0][i], packed[1][i]) for i in range(2))

    def ar_sum(k, p, own):
        ar_wait(k, p)
        terms = [own] + [(arb[k, p, j, 0:8], arb[k, p, j, 8:16]) for j in range(7)]
        while len(terms) > 1:
            terms = [pair_add(terms[i], terms[i + 1]) for i in range(0, len(terms), 2)]
        return terms[0]

    def solve(k, hi, idle):
        g = gram()
        for p in range(3):
            ar_start(k, p, g)
            if p == 0:
                idle()
            g = ar_sum(k, p, g)
        entries = []
        for e in range(14):
            r, base = e % 8, 64 * (e // 8)
            entries.append(tuple(jnp.broadcast_to(q[r:r + 1, base:base + 1], (8, 128)) for q in g))
        return coefficients(entries, hi)

    level(4, first_residual)
    basis(0, jnp.ones((1, 1), F32))
    best = ar_max(0, 2, best)
    hi1 = jnp.max(jnp.max(jnp.where(low, best, 0.0), axis=0, keepdims=True), axis=1, keepdims=True)
    hi2 = jnp.max(jnp.max(jnp.where(low, 0.0, best), axis=0, keepdims=True), axis=1, keepdims=True)
    for k in (1, 2, 3):
        basis(k, hi1)
    def keep_target():
        def plane(x, _):
            v0_s[x] = w_s[x]
            return 0

        lax.fori_loop(1, EX - 1, plane, 0)

    y1 = solve(1, jnp.broadcast_to(hi1, (8, 128)), keep_target)

    slots = [(lane >= 16 * y - 5) & (lane < 16 * y + 5) for y in range(8)]
    slots[0] = (lane < 5) | (lane >= 123)

    def update(x, _):
        ys = pl.ds(H, CY)
        v = w_s[H + x, ys, :, 0:128]
        for i in range(4):
            v = v + y1[i] * pk[i, H + x, ys, :, 0:128]
        w_s[H + x, ys, :, 0:128] = v
        v4[x] = v[:, 0:4, :]
        packed = v[0]
        for y in range(1, CY):
            packed = jnp.where(slots[y], pltpu.roll(v[y], 16 * y, 1), packed)
        zp[x] = packed[0:4, :]
        return 0

    for x in range(CX):
        update(x, 0)
    for o in order:
        v_copy(o).start()

    near_low = (lane & 15) < 8

    def take(dx, dy):
        (x0, nx), (y0, ny) = OWNED[dx], OWNED[dy]
        gy0 = GIVEN[-dy]
        g = group(dx, dy)
        for dz in (-1, 0, 1):
            if (dx, dy, dz) != (0, 0, 0):
                v_copy((-dx, -dy, -dz)).wait_recv()

        def plane(x, _):
            after = rz[g, 1, x]
            before = rz[g, 0, x]
            after = jnp.concatenate([after, after], axis=0)
            before = jnp.concatenate([before, before], axis=0)
            ends = jnp.where(near_low, after, before)
            for y in range(ny):
                sy = (128 - 16 * (gy0 + y)) % 128
                w_s[x0 + x, y0 + y, :, 128:256] = pltpu.roll(ends, sy, 1) if sy else ends
            ys = pl.ds(y0, ny)
            if (dx, dy) != (0, 0):
                head = rv[g, x, 0:ny]
                w_s[x0 + x, ys, :, 0:128] = jnp.concatenate([head, head], axis=1)
            f_s[x0 + x, ys] = a2_s[x0 + x, ys] * w_s[x0 + x, ys]
            return 0

        for x in range(nx):
            plane(x, 0)

    take(0, 0)
    for dx, dy in groups:
        take(dx, dy)

    level(4, second_residual)
    for k in range(4):
        basis(k, hi2)
    y2 = solve(2, jnp.broadcast_to(hi2, (8, 128)), lambda: None)
    y2 = [jnp.concatenate([q, q], axis=1) for q in y2]

    def finish(x, _):
        ys = pl.ds(H, CY + 1)
        v = w_s[H + x, ys]
        for i in range(4):
            v = v + y2[i] * pk[i, H + x, ys]
        w_s[H + x, ys] = v
        high = v.astype(BF16).astype(F32)
        vq[x * 9:x * 9 + 9] = jnp.where(low8, high, v - high)
        return 0

    for x in range(CX + 1):
        finish(x, 0)
    for f in range(3):
        for x in range(CX):
            for y in range(CY):
                v_out[f, x, y:y + 1, :] = w_s[H + x, H + y, f:f + 1, 0:128]

    ci, cj, ck = cells(13)
    for c in range(2):
        kt0[:, c * 128:(c + 1) * 128] = jnp.where(zrow == ck + c, 1.0, 0.0).astype(BF16)
    qg[...] = jnp.dot(vq[...].reshape(81 * 8, LANES).astype(BF16), kt0[:, 0:256],
                      preferred_element_type=F32).reshape(81, 8, LANES)
    ci = jnp.broadcast_to(jnp.concatenate([ci, ci], axis=1), (8, LANES))
    cj = jnp.broadcast_to(jnp.concatenate([cj, cj], axis=1), (8, LANES))
    corner = {}
    for a in range(2):
        at_x = []
        for y in range(9):
            z = qg[a * 9 + y]
            for x in range(1, 8):
                z = jnp.where(ci == x, qg[(x + a) * 9 + y], z)
            at_x.append(z)
        for b in range(2):
            z = at_x[b]
            for y in range(1, 8):
                z = jnp.where(cj == y, at_x[y + b], z)
            corner[a, b] = z + pltpu.roll(z, 4, 0)

    def points(i, _):
        at = pl.ds(pl.multiple_of(i * 8, 8), 8)
        fx, fy, fz = tr[0, at], tr[1, at], tr[2, at]
        gx, gy, gz = 1.0 - fx, 1.0 - fy, 1.0 - fz
        w = {(0, 0): gx * gy, (0, 1): gx * fy, (1, 0): fx * gy, (1, 1): fx * fy}
        for f in range(3):
            total = None
            for key, wt in w.items():
                r = corner[key]
                term = wt * (gz * r[f:f + 1, 0:128] + fz * r[f:f + 1, 128:256])
                total = term if total is None else total + term
            ut[f, at] = total
        return 0

    lax.fori_loop(0, PTS // 8, points, 0)
    for f in range(3):
        u_out[f] = ut[f].T

    for o in order:
        deposit_copy(o).wait_send()
        v_copy(o).wait_send()
    for k in range(3):
        for p in range(3):
            pltpu.make_async_copy(arb.at[k, p], arb.at[k, p], ar_ss.at[k, p]).wait()


def shards(point_offset, point_mass, point_velocity, point_stiffness, cell_index, live_count):
    vm = pl.BlockSpec(memory_space=pltpu.VMEM)
    ext = pltpu.VMEM((EX, EX, 8, LANES), F32)
    v, u = pl.pallas_call(
        kernel,
        out_shape=(jax.ShapeDtypeStruct((3, CX, CY, CZ), F32), jax.ShapeDtypeStruct((3, NB, PTS), F32)),
        in_specs=[vm] * 6,
        out_specs=(vm, vm),
        scratch_shapes=[
            pltpu.VMEM((8, PTS, NB), F32),
            pltpu.VMEM((27, 48, NB), F32),
            pltpu.VMEM((LANES, 768), BF16),
            pltpu.VMEM((LANES, 768), BF16),
            pltpu.VMEM((81, 16, 768), BF16),
            pltpu.VMEM((81, 16, 768), BF16),
            ext, ext, ext, ext, ext, ext, ext, ext, ext, ext, ext,
            pltpu.VMEM((4, EX, EX, 8, LANES), F32),
            pltpu.VMEM((CX, CY, 8, CZ), F32),
            pltpu.VMEM((CX, CY, 4, CZ), F32),
            pltpu.VMEM((CX, 4, CZ), F32),
            pltpu.VMEM((9, CX, CY, 4, CZ), F32),
            pltpu.VMEM((9, 2, CX, 4, CZ), F32),
            pltpu.VMEM((3, 3, 16, 128), F32),
            pltpu.VMEM((3, 3, 7, 16, 128), F32),
            pltpu.VMEM((3, PTS, NB), F32),
            pltpu.VMEM((81, 8, LANES), F32),
            pltpu.VMEM((81, 8, LANES), F32),
            pltpu.SemaphoreType.DMA((27,)),
            pltpu.SemaphoreType.DMA((27,)),
            pltpu.SemaphoreType.DMA((27,)),
            pltpu.SemaphoreType.DMA((27,)),
            pltpu.SemaphoreType.DMA((3, 3)),
            pltpu.SemaphoreType.DMA((3, 3)),
        ],
        compiler_params=pltpu.CompilerParams(
            collective_id=0, has_side_effects=True, vmem_limit_bytes=60 << 20),
        name="granular_step",
    )(
        point_offset.reshape(3, NB, PTS),
        point_mass.reshape(NB, PTS),
        point_velocity.reshape(3, NB, PTS),
        point_stiffness.reshape(NB, PTS),
        cell_index.reshape(1, NB),
        live_count.reshape(1, NB),
    )
    return v, u.reshape(3, 1, 1, 1, NB, PTS)


def solution(mesh):
    return jax.shard_map(
        shards,
        mesh=mesh,
        in_specs=(
            P(None, "gx", "gy", "gz", None, None),
            P("gx", "gy", "gz", None, None),
            P(None, "gx", "gy", "gz", None, None),
            P("gx", "gy", "gz", None, None),
            P("gx", "gy", "gz", None),
            P("gx", "gy", "gz", None),
        ),
        out_specs=(P(None, "gx", "gy", "gz"), P(None, "gx", "gy", "gz", None, None)),
        check_vma=False,
    )
```

```python
import functools
import itertools

import jax
import jax.numpy as jnp
from jax import lax
from jax.experimental import pallas as pl
from jax.experimental.pallas import tpu as pltpu
from jax.sharding import PartitionSpec as P

CX = 8
CY = 8
CZ = 128
NB = 128
PTS = 128
N = 8
H = 5
EX = CX + 2 * H
LANES = 2 * CZ
AXES = ("gx", "gy", "gz")
MESH = pl.DeviceIdType.MESH
F32 = jnp.float32
BF16 = jnp.bfloat16
C_ALL = 0.25 * (6.0 + 12.0 / 2.0 + 8.0 / 3.0)
SHIFTS = (0.0, 0.85, 0.45, 0.2)
SCALE = 2.0 ** 15
PEERS = (4, 3, 5, 2, 6, 1, 7)
PAIRS = [(i, j) for i in range(4) for j in range(i, 5)]
NEAR = [o for o in itertools.product((-1, 0, 1), repeat=3) if any(o)]


def slot(o):
    return (o[0] + 1) * 9 + (o[1] + 1) * 3 + (o[2] + 1)


def group(dx, dy):
    return (dx + 1) * 3 + (dy + 1)


REACH = {-1: (0, H + 1), 0: (H, CX + 1), 1: (H + CX, H)}
OWNED = {-1: (0, H), 0: (H, CX), 1: (H + CX, H)}
GIVEN = {-1: 0, 0: 0, 1: CX - H}


def two_sum(a, b):
    s = a + b
    t = s - a
    return s, (a - (s - t)) + (b - t)


def quick_sum(a, b):
    s = a + b
    return s, b - (s - a)


def split(a):
    t = a * 4097.0
    high = t - (t - a)
    return high, a - high


def prod_error(p, a, b):
    return ((a[0] * b[0] - p) + a[0] * b[1] + a[1] * b[0]) + a[1] * b[1]


def pair_add(a, b):
    s, e = two_sum(a[0], b[0])
    return quick_sum(s, e + (a[1] + b[1]))


def pair_mul(a, b):
    p = a[0] * b[0]
    e = prod_error(p, split(a[0]), split(b[0]))
    return quick_sum(p, e + (a[0] * b[1] + a[1] * b[0]))


def pair_div(a, b):
    q = a[0] / b[0]
    qb = pair_mul((q, jnp.zeros_like(q)), b)
    r = pair_add(a, (-qb[0], -qb[1]))
    return quick_sum(q, r[0] / b[0])


def coefficients(gram, theta, tau):
    zero = jnp.zeros_like(gram[0][0])
    g = {}
    for e, (i, j) in enumerate(PAIRS):
        g[i, j] = gram[e]
    d, l = [], {}
    for j in range(4):
        piv = g[j, j]
        floor = jnp.maximum(gram[PAIRS.index((j, j))][0] * 1e-13, 1e-36)
        bad = piv[0] < floor
        piv = (jnp.where(bad, floor, piv[0]), jnp.where(bad, zero, piv[1]))
        d.append(piv)
        for k in range(j + 1, 5):
            l[j, k] = pair_div(g[j, k], piv)
        for i in range(j + 1, 4):
            for k in range(i, 5):
                m = pair_mul(l[j, i], g[j, k])
                g[i, k] = pair_add(g[i, k], (-m[0], -m[1]))
    low = {key: val[0] for key, val in l.items()}
    a = [theta[0] + tau[0] * low[0, 1]]
    for j in (1, 2, 3):
        a.append(theta[j] + (tau[j] * low[j, j + 1] - tau[j - 1] * low[j - 1, j]))
    ratio = [None] + [d[j][0] / d[j - 1][0] for j in (1, 2, 3)]
    c = [jnp.maximum(a[0], 1.0)]
    for j in (1, 2, 3):
        c.append(jnp.maximum(a[j] - tau[j - 1] * tau[j - 1] * ratio[j] / c[j - 1], 1.0))
    f = [jnp.ones_like(zero)]
    for j in (1, 2, 3):
        f.append(-(tau[j - 1] * f[j - 1]) / c[j - 1])
    z = [None] * 4
    z[3] = f[3] / c[3]
    for j in (2, 1, 0):
        z[j] = (f[j] - tau[j] * ratio[j + 1] * z[j + 1]) / c[j]
    y = [None] * 4
    y[3] = z[3]
    y[2] = z[2] - low[2, 3] * y[3]
    y[1] = z[1] - low[1, 2] * y[2] - low[1, 3] * y[3]
    y[0] = z[0] - low[0, 1] * y[1] - low[0, 2] * y[2] - low[0, 3] * y[3]
    return y


def kernel(off, mass, vel, stiff, cell, live, v_out, u_out,
           tr, rx, kt0, kt1, am0, am1, dep, w_s, v0_s, a1_s, a2_s, mb_s, d_s, e_s, f_s, gs, ns, pk, p4,
           v4, zp, rv, rz, ars, arb, vq, qg,
           dep_ss, dep_rs, v_ss, v_rs, ar_ss, ar_rs):
    me = [lax.axis_index(a) for a in AXES]
    kts, ams = (kt0, kt1), (am0, am1)

    def peer(o):
        return tuple(m if q == 0 else lax.rem(m + (q % N), N) for m, q in zip(me, o))

    rx[:, 40:48, :] = jnp.zeros((27, 8, NB), F32)
    greeted = set((o[0] % N, o[1] % N, o[2] % N) for o in NEAR)
    for axis in range(3):
        for q in PEERS:
            greeted.add(tuple(q if i == axis else 0 for i in range(3)))
    barrier = pltpu.get_barrier_semaphore()
    for o in sorted(greeted):
        pl.semaphore_signal(barrier, inc=1, device_id=peer(o), device_id_type=MESH)

    row = lax.broadcasted_iota(jnp.int32, (8, LANES), 0)
    low8 = row < 4
    empty = (row & 3) == 3
    low = lax.broadcasted_iota(jnp.int32, (8, 128), 0) < 4
    lane = lax.broadcasted_iota(jnp.int32, (8, 128), 1)
    rows8 = lax.broadcasted_iota(jnp.int32, (8, 128), 0)

    keep = lax.broadcasted_iota(jnp.int32, (PTS, NB), 0) < live[...]
    for i in range(3):
        tr[i] = off[i].T
        tr[3 + i] = vel[i].T
    tr[6] = jnp.where(keep, stiff[...].T, 0.0)
    tr[7] = jnp.where(keep, mass[...].T, 0.0)

    def sums(i, acc):
        at = pl.ds(pl.multiple_of(i * 8, 8), 8)
        fx, fy, fz = tr[0, at], tr[1, at], tr[2, at]
        m = tr[7, at]
        data = [m * tr[3, at], m * tr[4, at], m * tr[5, at], tr[6, at], m]
        new = []
        for wx in (1.0 - fx, fx):
            for wy in (1.0 - fy, fy):
                wxy = wx * wy
                for wz in (1.0 - fz, fz):
                    wt = wxy * wz
                    for value in data:
                        new.append(acc[len(new)] + wt * value)
        return tuple(new)

    acc = lax.fori_loop(0, PTS // 8, sums, tuple(jnp.zeros((8, NB), F32) for _ in range(40)))
    for e in range(40):
        rx[13, e:e + 1, :] = jnp.sum(acc[e], axis=0, keepdims=True)
    rx[13, 40:41, :] = cell[...].astype(F32)

    pl.semaphore_wait(barrier, len(greeted))

    def neg(o):
        return tuple(-q for q in o)

    def deposit_copy(o):
        return pltpu.make_async_remote_copy(
            src_ref=rx.at[13, pl.ds(0, 41)], dst_ref=rx.at[slot(neg(o)), pl.ds(0, 41)], send_sem=dep_ss.at[slot(o)],
            recv_sem=dep_rs.at[slot(neg(o))], device_id=peer(o), device_id_type=MESH)

    def v_copy(o):
        if o[2] == 0:
            gx0, gy0 = GIVEN[o[0]], GIVEN[o[1]]
            nx, ny = OWNED[-o[0]][1], OWNED[-o[1]][1]
            src = v4.at[pl.ds(gx0, nx), pl.ds(gy0, ny)]
            dst = rv.at[group(-o[0], -o[1]), pl.ds(0, nx), pl.ds(0, ny)]
        else:
            gx0, nx = GIVEN[o[0]], OWNED[-o[0]][1]
            src = zp.at[pl.ds(gx0, nx)]
            dst = rz.at[group(-o[0], -o[1]), (1 - o[2]) // 2, pl.ds(0, nx)]
        return pltpu.make_async_remote_copy(
            src_ref=src, dst_ref=dst, send_sem=v_ss.at[slot(o)], recv_sem=v_rs.at[slot(neg(o))],
            device_id=peer(o), device_id_type=MESH)

    def ar_start(k, p, value):
        ars[k, p, 0:8] = value[0]
        ars[k, p, 8:16] = value[1]
        for j, q in enumerate(PEERS):
            axis = 2 - p
            pltpu.make_async_remote_copy(
                src_ref=ars.at[k, p], dst_ref=arb.at[k, p, j], send_sem=ar_ss.at[k, p],
                recv_sem=ar_rs.at[k, p], device_id=peer(tuple(q if i == axis else 0 for i in range(3))),
                device_id_type=MESH).start()

    def ar_wait(k, p):
        pltpu.make_async_copy(arb.at[k, p], arb.at[k, p], ar_rs.at[k, p]).wait()

    order = sorted(NEAR, key=lambda o: -sum(abs(q) for q in o))
    for o in order:
        deposit_copy(o).start()

    zrow = lax.broadcasted_iota(jnp.int32, (LANES, NB), 0)
    zrow = jnp.where(zrow >= 192, zrow - LANES, zrow)

    def cells(n):
        c = rx[n, 40:41, :].astype(jnp.int32)
        return c >> 10, (c >> 7) & 7, c & 127

    def add_group(dx, dy, zs, which):
        kt, am = kts[which], ams[which]
        (x0, nx), (y0, ny) = REACH[dx], REACH[dy]
        width = 256 * len(zs)
        for zi, dz in enumerate(zs):
            n = slot((dx, dy, dz))
            ci, cj, ck = cells(n)
            for c in range(2):
                at = pl.ds((zi * 2 + c) * 128, 128)
                kt[:, at] = jnp.where(zrow == ck + (c + CZ * dz), 1.0, 0.0).astype(BF16)
                ys, xs = [], []
                for b in range(2):
                    plane = lax.broadcasted_iota(jnp.int32, (ny, 16, NB), 0)
                    ys.append(jnp.where(plane == cj + (b + 8 * dy + H - y0), 1.0, 0.0).astype(BF16))
                    plane = lax.broadcasted_iota(jnp.int32, (nx, 16, NB), 0)
                    xs.append(jnp.where(plane == ci + (b + 8 * dx + H - x0), 1.0, 0.0).astype(BF16))
                total = None
                for a in range(2):
                    u = None
                    for b in range(2):
                        e = a * 4 + b * 2 + c
                        s = rx[n, 5 * e:5 * e + 8, :]
                        high = s.astype(BF16).astype(F32)
                        s16 = jnp.concatenate([high, s - high], axis=0).astype(BF16)
                        term = ys[b] * s16
                        u = term if u is None else u + term
                    term = xs[a].reshape(nx, 1, 16, NB) * u.reshape(1, ny, 16, NB)
                    total = term if total is None else total + term
                am[0:nx * ny, :, at] = total.reshape(nx * ny, 16, NB)
        lhs = am[0:nx * ny, :, 0:width].reshape(nx * ny * 16, width)
        out = lax.dot_general(lhs, kt[:, 0:width], (((1,), (1,)), ((), ())), preferred_element_type=F32)
        out = out.reshape(nx, ny, 16, LANES)
        dep[x0:x0 + nx, y0:y0 + ny] += out[:, :, 0:8] + out[:, :, 8:16]

    dep[...] = jnp.zeros((EX, EX, 8, LANES), F32)
    add_group(0, 0, (0,), 1)

    def node(x, ys):
        t = dep[x, ys]
        mb = jnp.broadcast_to(dep[x, ys, 4:5, :], t.shape) + 1.0
        sb = jnp.broadcast_to(dep[x, ys, 3:4, :], t.shape) + 0.1
        dup = jnp.where(low8, t, pltpu.roll(t, 4, 1))
        return jnp.where(empty, 0.0, dup / mb), mb, sb

    def wait_group(dx, dy):
        for dz in (-1, 0, 1):
            if (dx, dy, dz) != (0, 0, 0):
                deposit_copy((-dx, -dy, -dz)).wait_recv()

    wait_group(0, 0)
    add_group(0, 0, (-1, 1), 0)
    groups = [(-1, 0), (1, 0), (0, -1), (0, 1), (-1, -1), (-1, 1), (1, -1), (1, 1)]
    for i, (dx, dy) in enumerate(groups):
        wait_group(dx, dy)
        add_group(dx, dy, (-1, 0, 1), (i + 1) % 2)

    def coefs(x, _):
        v, mb, sb = node(x, pl.ds(0, EX))
        a2 = jnp.where(low8, 0.125, 0.125 * sb)
        w_s[x] = v
        mb_s[x] = mb
        a1_s[x] = jnp.where(low8, sb, 1.0)
        a2_s[x] = a2
        d_s[x] = C_ALL * sb
        f_s[x] = jnp.where(row == 3, 0.125 * sb, a2 * v)
        return 0

    for x in range(EX):
        coefs(x, 0)

    def level(k, emit):
        first, last = H - k, H + CX + k
        ys = pl.ds(first, last - first)
        wide = pl.ds(0, LANES if k else CZ)
        for x in range(first - 1, last + 1):
            f = f_s[x, first - 1:last + 1]
            sz = pltpu.roll(f, 1, 2) + pltpu.roll(f, LANES - 1, 2)
            if not k:
                f, sz = f[:, :, 0:CZ], sz[:, :, 0:CZ]
            h0, h1, h2 = sz + sz, f + f + sz, f + (2.0 / 3.0) * sz
            gs[x, ys, :, wide] = h1[1:-1] + (h2[:-2] + h2[2:])
            ns[x, ys, :, wide] = h0[1:-1] + (h1[:-2] + h1[2:])
        for x in range(first, last):
            emit(x, ys, ns[x, ys, :, wide] + (gs[x - 1, ys, :, wide] + gs[x + 1, ys, :, wide]))

    def folded(x, ys, sums, wide):
        q = a1_s[x, ys, :, wide] * sums
        return q + pltpu.roll(q, 4, 1)

    full = pl.ds(0, LANES)

    def first_residual(x, ys, sums):
        d = d_s[x, ys] + jnp.broadcast_to(sums[:, 3:4, :], sums.shape)
        d_s[x, ys] = d
        lq = folded(x, ys, sums, full)
        v = w_s[x, ys]
        mb = mb_s[x, ys]
        mvv = mb * v * v
        e_s[x, ys] = mb + 0.9 * mvv + d
        p = jnp.where(empty, 0.0, lq - (d + 0.3 * mvv) * v)
        if H <= x < H + CX:
            own = slice(4, 4 + CY)
            vo, mo, do = v[own, :, 0:CZ], mb[own, :, 0:CZ], d[own, :, 0:CZ]
            vv = vo * vo
            damped = vo * (1.0 + 0.6 * vv) / (1.0 + 0.9 * vv)
            largest.append(jnp.max(mo * (1.0 + 0.9 * damped * damped) + do, axis=0))
        pk[0, x, ys] = p
        f_s[x, ys] = a2_s[x, ys] * p

    def second_residual(x, ys, sums):
        d = d_s[x, ys]
        lq = folded(x, ys, sums, full)
        v = w_s[x, ys]
        mb = mb_s[x, ys]
        mvv = mb * v * v
        e_s[x, ys] = mb + 0.9 * mvv + d
        p = lq - (d + 0.3 * mvv) * v - mb * (v - v0_s[x, ys])
        pk[0, x, ys] = p
        f_s[x, ys] = a2_s[x, ys] * p

    def basis(k, shift, factor):
        lanes = CZ if k == 3 else LANES
        wide = pl.ds(0, lanes)
        if shift is not None:
            shift = jnp.broadcast_to(shift, (8, lanes))
        factor = jnp.broadcast_to(factor, (8, lanes))

        def emit(x, ys, sums):
            lq = folded(x, ys, sums, wide)
            e = e_s[x, ys, :, wide]
            if shift is not None:
                e = e - shift
            p = (e * pk[k, x, ys, :, wide] - lq) * factor
            if k == 3:
                p4[x - H] = p
            else:
                pk[k + 1, x, ys] = p
                f_s[x, ys] = a2_s[x, ys] * p

        level(3 - k, emit)

    def gram():
        def plane(x, carry):
            acc = list(carry)
            for y in range(4):
                p = [jnp.where(low, pk[i, H + x, H + y, :, 0:128], pk[i, H + x, H + 4 + y, :, 0:128]) for i in range(4)]
                p.append(jnp.where(low, p4[x, y], p4[x, y + 4]))
                parts = [split(q) for q in p]
                for e, (i, j) in enumerate(PAIRS):
                    m = p[i] * p[j]
                    err = prod_error(m, parts[i], parts[j])
                    s, t = two_sum(acc[2 * e], m)
                    acc[2 * e] = s
                    acc[2 * e + 1] = acc[2 * e + 1] + (t + err)
            return tuple(acc)

        acc = lax.fori_loop(0, CX, plane, tuple(jnp.zeros((8, 128), F32) for _ in range(28)), unroll=2)
        packed = []
        for part in range(2):
            high = jnp.zeros((8, 128), F32)
            rest = jnp.zeros((8, 128), F32)
            for r in range(8):
                e = part * 8 + r
                if e >= 14:
                    continue
                a = (acc[2 * e], acc[2 * e + 1])
                for s in (4, 2, 1):
                    a = pair_add(a, (pltpu.roll(a[0], s, 0), pltpu.roll(a[1], s, 0)))
                high = jnp.where(rows8 == r, a[0], high)
                rest = jnp.where(rows8 == r, a[1], rest)
            a = (high, rest)
            for s in (64, 32, 16, 8, 4, 2, 1):
                a = pair_add(a, (pltpu.roll(a[0], s, 1), pltpu.roll(a[1], s, 1)))
            packed.append(a)
        return tuple(jnp.where(lane < 64, packed[0][i], packed[1][i]) for i in range(2))

    extra = (rows8 == 7) & (lane >= 64)

    def ar_sum(k, p, own):
        ar_wait(k, p)
        terms = [own] + [(arb[k, p, j, 0:8], arb[k, p, j, 8:16]) for j in range(7)]
        while len(terms) > 1:
            terms = [pair_add(terms[i], terms[i + 1]) for i in range(0, len(terms), 2)]
        if k:
            return terms[0]
        best = own[0]
        for j in range(7):
            best = jnp.maximum(best, arb[k, p, j, 0:8])
        return jnp.where(extra, best, terms[0][0]), jnp.where(extra, 0.0, terms[0][1])

    def solve(k, g, idle):
        for p in range(3):
            ar_start(k, p, g)
            if p == 0:
                idle()
            g = ar_sum(k, p, g)
        entries = []
        for e in range(14):
            r, base = e % 8, 64 * (e // 8)
            entries.append(tuple(jnp.broadcast_to(q[r:r + 1, base:base + 1], (8, 128)) for q in g))
        return entries, g

    largest = []
    level(4, first_residual)
    for k in range(4):
        basis(k, None, jnp.full((1, 1), 1.0 / SCALE, F32))

    def keep_target():
        def plane(x, _):
            v0_s[x] = w_s[x]
            return 0

        lax.fori_loop(1, EX - 1, plane, 0)

    best = functools.reduce(jnp.maximum, largest)
    best = jnp.max(jnp.max(best, axis=0, keepdims=True), axis=1, keepdims=True)
    g = gram()
    g = (jnp.where(extra, jnp.broadcast_to(best, (8, 128)), g[0]), g[1])
    entries, g = solve(0, g, keep_target)
    hi2 = g[0][7:8, 64:65]
    same = [jnp.full((8, 128), SCALE, F32)] * 4
    y1 = coefficients(entries, [0.0] * 4, same)

    slots = [(lane >= 16 * y - 5) & (lane < 16 * y + 5) for y in range(8)]
    slots[0] = (lane < 5) | (lane >= 123)

    def update(x, _):
        ys = pl.ds(H, CY)
        v = w_s[H + x, ys, :, 0:128]
        for i in range(4):
            v = v + y1[i] * pk[i, H + x, ys, :, 0:128]
        w_s[H + x, ys, :, 0:128] = v
        v4[x] = v[:, 0:4, :]
        packed = v[0]
        for y in range(1, CY):
            packed = jnp.where(slots[y], pltpu.roll(v[y], 16 * y, 1), packed)
        zp[x] = packed[0:4, :]
        return 0

    for x in range(CX):
        update(x, 0)
    for o in order:
        v_copy(o).start()

    near_low = (lane & 15) < 8

    def take(dx, dy):
        (x0, nx), (y0, ny) = OWNED[dx], OWNED[dy]
        gy0 = GIVEN[-dy]
        g = group(dx, dy)
        for dz in (-1, 0, 1):
            if (dx, dy, dz) != (0, 0, 0):
                v_copy((-dx, -dy, -dz)).wait_recv()

        def plane(x, _):
            after = rz[g, 1, x]
            before = rz[g, 0, x]
            after = jnp.concatenate([after, after], axis=0)
            before = jnp.concatenate([before, before], axis=0)
            ends = jnp.where(near_low, after, before)
            for y in range(ny):
                sy = (128 - 16 * (gy0 + y)) % 128
                w_s[x0 + x, y0 + y, :, 128:256] = pltpu.roll(ends, sy, 1) if sy else ends
            ys = pl.ds(y0, ny)
            if (dx, dy) != (0, 0):
                head = rv[g, x, 0:ny]
                w_s[x0 + x, ys, :, 0:128] = jnp.concatenate([head, head], axis=1)
            f_s[x0 + x, ys] = a2_s[x0 + x, ys] * w_s[x0 + x, ys]
            return 0

        for x in range(nx):
            plane(x, 0)

    take(0, 0)
    for dx, dy in groups:
        take(dx, dy)

    level(4, second_residual)
    for k in range(4):
        basis(k, hi2 * SHIFTS[k] if k else None, 2.0 / hi2 if k else jnp.ones((1, 1), F32))
    entries, _ = solve(1, gram(), lambda: None)
    hi2 = jnp.broadcast_to(hi2, (8, 128))
    y2 = coefficients(entries, [hi2 * s for s in SHIFTS], [jnp.ones((8, 128), F32)] + [hi2 * 0.5] * 3)
    y2 = [jnp.concatenate([q, q], axis=1) for q in y2]

    def finish(x, _):
        ys = pl.ds(H, CY + 1)
        v = w_s[H + x, ys]
        for i in range(4):
            v = v + y2[i] * pk[i, H + x, ys]
        w_s[H + x, ys] = v
        high = v.astype(BF16).astype(F32)
        vq[x * 9:x * 9 + 9] = jnp.where(low8, high, v - high)
        return 0

    for x in range(CX + 1):
        finish(x, 0)
    for f in range(3):
        for x in range(CX):
            for y in range(CY):
                v_out[f, x, y:y + 1, :] = w_s[H + x, H + y, f:f + 1, 0:128]

    ci, cj, ck = cells(13)
    for c in range(2):
        kt0[:, c * 128:(c + 1) * 128] = jnp.where(zrow == ck + c, 1.0, 0.0).astype(BF16)
    qg[...] = jnp.dot(vq[...].reshape(81 * 8, LANES).astype(BF16), kt0[:, 0:256],
                      preferred_element_type=F32).reshape(81, 8, LANES)
    ci = jnp.broadcast_to(jnp.concatenate([ci, ci], axis=1), (8, LANES))
    cj = jnp.broadcast_to(jnp.concatenate([cj, cj], axis=1), (8, LANES))
    corner = {}
    for a in range(2):
        at_x = []
        for y in range(9):
            z = qg[a * 9 + y]
            for x in range(1, 8):
                z = jnp.where(ci == x, qg[(x + a) * 9 + y], z)
            at_x.append(z)
        for b in range(2):
            z = at_x[b]
            for y in range(1, 8):
                z = jnp.where(cj == y, at_x[y + b], z)
            corner[a, b] = z + pltpu.roll(z, 4, 0)

    def points(i, _):
        at = pl.ds(pl.multiple_of(i * 8, 8), 8)
        fx, fy, fz = tr[0, at], tr[1, at], tr[2, at]
        gx, gy, gz = 1.0 - fx, 1.0 - fy, 1.0 - fz
        w = {(0, 0): gx * gy, (0, 1): gx * fy, (1, 0): fx * gy, (1, 1): fx * fy}
        for f in range(3):
            total = None
            for key, wt in w.items():
                r = corner[key]
                term = wt * (gz * r[f:f + 1, 0:128] + fz * r[f:f + 1, 128:256])
                total = term if total is None else total + term
            u_out[f, at] = total
        return 0

    lax.fori_loop(0, PTS // 8, points, 0)
    for o in order:
        deposit_copy(o).wait_send()
        v_copy(o).wait_send()
    for k in range(2):
        for p in range(3):
            pltpu.make_async_copy(arb.at[k, p], arb.at[k, p], ar_ss.at[k, p]).wait()


def shards(point_offset, point_mass, point_velocity, point_stiffness, cell_index, live_count):
    vm = pl.BlockSpec(memory_space=pltpu.VMEM)
    ext = pltpu.VMEM((EX, EX, 8, LANES), F32)
    v, u = pl.pallas_call(
        kernel,
        out_shape=(jax.ShapeDtypeStruct((3, CX, CY, CZ), F32), jax.ShapeDtypeStruct((3, PTS, NB), F32)),
        in_specs=[vm] * 6,
        out_specs=(vm, vm),
        scratch_shapes=[
            pltpu.VMEM((8, PTS, NB), F32),
            pltpu.VMEM((27, 48, NB), F32),
            pltpu.VMEM((LANES, 768), BF16),
            pltpu.VMEM((LANES, 768), BF16),
            pltpu.VMEM((81, 16, 768), BF16),
            pltpu.VMEM((81, 16, 768), BF16),
            ext, ext, ext, ext, ext, ext, ext, ext, ext, ext, ext,
            pltpu.VMEM((4, EX, EX, 8, LANES), F32),
            pltpu.VMEM((CX, CY, 8, CZ), F32),
            pltpu.VMEM((CX, CY, 4, CZ), F32),
            pltpu.VMEM((CX, 4, CZ), F32),
            pltpu.VMEM((9, CX, CY, 4, CZ), F32),
            pltpu.VMEM((9, 2, CX, 4, CZ), F32),
            pltpu.VMEM((2, 3, 16, 128), F32),
            pltpu.VMEM((2, 3, 7, 16, 128), F32),
            pltpu.VMEM((81, 8, LANES), F32),
            pltpu.VMEM((81, 8, LANES), F32),
            pltpu.SemaphoreType.DMA((27,)),
            pltpu.SemaphoreType.DMA((27,)),
            pltpu.SemaphoreType.DMA((27,)),
            pltpu.SemaphoreType.DMA((27,)),
            pltpu.SemaphoreType.DMA((2, 3)),
            pltpu.SemaphoreType.DMA((2, 3)),
        ],
        compiler_params=pltpu.CompilerParams(
            collective_id=0, has_side_effects=True, vmem_limit_bytes=60 << 20),
        name="granular_step",
    )(
        point_offset.reshape(3, NB, PTS),
        point_mass.reshape(NB, PTS),
        point_velocity.reshape(3, NB, PTS),
        point_stiffness.reshape(NB, PTS),
        cell_index.reshape(1, NB),
        live_count.reshape(1, NB),
    )
    return v, u.transpose(0, 2, 1).reshape(3, 1, 1, 1, NB, PTS)


def solution(mesh):
    return jax.shard_map(
        shards,
        mesh=mesh,
        in_specs=(
            P(None, "gx", "gy", "gz", None, None),
            P("gx", "gy", "gz", None, None),
            P(None, "gx", "gy", "gz", None, None),
            P("gx", "gy", "gz", None, None),
            P("gx", "gy", "gz", None),
            P("gx", "gy", "gz", None),
        ),
        out_specs=(P(None, "gx", "gy", "gz"), P(None, "gx", "gy", "gz", None, None)),
        check_vma=False,
    )
```
